256 devices in a mesh: frame: 128 (over z, x, y), track: 2 (over core).
Axes of the slice: x: 4, y: 4, z: 8, core: 2. Of those that a mesh axis runs over, the one named last changes fastest.
Arguments:
- feature_maps: bfloat16 [256, 4096, 256], P('frame'), may hold values from -16 to 16
- query_frame: int32 [1024], P('track'), may hold values from 0 to 255
- query_pixel: int32 [2, 1024], P(None, 'track'), may hold values from 0 to 63
- conv_kernel: float32 [3, 512], replicated, may hold values from -3 to 3
- norm_gain: float32 [512], replicated, may hold values from 0.5 to 1.5
- w_in: bfloat16 [2048, 512], P('track'), may hold values from -0.25 to 0.25
- w_out: bfloat16 [2048, 256], P('track'), may hold values from -0.125 to 0.125
Outputs:
- coarse_points: float32 [2, 256, 1024], P(None, 'frame', 'track')
- refined_points: float32 [2, 256, 1024], P(None, 'frame', 'track')
The draws below stay inside these ranges and needn't reach their ends.
All inputs are finite; a program needn't handle non-finite values.
Results may differ from the reference program's by a relative error of at most 0.0035.
The reference program's roundings to bfloat16 on the way (of `queries`, `sampled`, `normed`, `hidden` and `updated`) count: a program that leaves them out, or rounds other values in their place, can miss the bound.
Values may be sent and summed in bfloat16 or wider, within the bound.
A program may use at most 128 MiB of HBM per device.

```python
import math
import jax
import jax.numpy as jnp
import numpy as np
from jax import lax

C = 256
HID = 2048
SIDE = 64
KT = 3
TR_DEV = 4
HW = 4096
MIX = 512
FRAMES = 256
TRACKS = 1024


def draw_feature_maps(key, part):
    first_key = jax.random.fold_in(jax.random.fold_in(key, 17), 0)
    values = jnp.clip(jax.random.normal(first_key, (FRAMES, HW, C), jnp.float32), -4.0, 4.0)
    return values.astype(jnp.bfloat16)


def set_ends(values, stream_key, smallest, top_value):
    shape = values.shape
    place = [jax.random.randint(jax.random.fold_in(stream_key, axis), (), 0, shape[axis]) for axis in range(len(shape))]
    values = values.at[tuple(place)].set(smallest)
    longest = shape.index(max(shape))
    place[longest] = (place[longest] + 1) % shape[longest]
    return values.at[tuple(place)].set(top_value)


def shard_levels(stream_key, dims, cuts, low, top_value):
    def one(axis_at, shards_of):
        draws = jax.random.uniform(jax.random.fold_in(jax.random.fold_in(stream_key, 6), axis_at), (shards_of,), jnp.float32, low / len(cuts), top_value / len(cuts))
        return jnp.repeat(jnp.exp(draws), dims[axis_at] // shards_of).reshape((-1,) + (1,) * (len(dims) - axis_at - 1))

    factor_of = one(*cuts[0])
    for cut in cuts[1:]:
        factor_of = factor_of * one(*cut)
    return factor_of


def rank_bounds(count, slope):
    weights = [(1 << 20) // math.isqrt(rank ** slope) + 1 for rank in range(1, count + 1)]
    spread = 1 + sum(weights) // (1 << 30)
    return np.cumsum(np.array([max(1, weight // spread) for weight in weights]))


def ranked(stream_key, shape, amount, lean):
    listing = rank_bounds(amount, lean)
    ticket = jax.random.randint(jax.random.fold_in(stream_key, 1), shape, 0, int(listing[amount - 1]))
    grade = jnp.searchsorted(jnp.asarray(listing, jnp.int32), ticket, side="right")
    return jax.random.permutation(jax.random.fold_in(stream_key, 2), amount)[grade].astype(jnp.int32)


def normal_values(key, extent, width, limit, shards=(), kind=jnp.bfloat16):
    gain = shard_levels(key, extent, shards, -0.22, 0.18) if shards else 1.0
    values = jax.random.normal(key, extent, jnp.float32) * width * gain
    return jnp.minimum(jnp.maximum(values, -limit), limit).astype(kind)


def setup_inputs(seed: int = 0) -> dict:
    arg_keys = jax.random.split(jax.random.key(seed), 8)
    return {
        "feature_maps": draw_feature_maps(jax.random.fold_in(arg_keys[7], 71), 0),
        "query_frame": set_ends(ranked(arg_keys[1], (TRACKS,), FRAMES, 2), jax.random.fold_in(arg_keys[1], 3), 0, FRAMES - 1).astype(jnp.int32),
        "query_pixel": set_ends(jax.random.randint(arg_keys[2], (2, TRACKS), 0, SIDE), jax.random.fold_in(arg_keys[2], 1), 0, SIDE - 1).astype(jnp.int32),
        "conv_kernel": normal_values(arg_keys[3], (KT, MIX), 0.6, 3.0, (), jnp.float32),
        "norm_gain": jnp.clip(1.0 + 0.1 * jax.random.normal(arg_keys[4], (MIX,), jnp.float32), 0.5, 1.5),
        "w_in": normal_values(arg_keys[5], (HID, MIX), MIX ** -0.5, 0.25, ((0, 2),)),
        "w_out": normal_values(arg_keys[6], (HID, C), HID ** -0.5, 0.125, ((0, 2),)),
    }


def soft_argmax(queries, frame_map):
    scores = jnp.einsum('tc,pc->tp', queries.astype(jnp.float32), frame_map.astype(jnp.float32)) * C ** (-0.5)
    peak = lax.optimization_barrier(jnp.max(scores, axis=1, keepdims=True))
    expo = jnp.exp(scores - peak)
    weights = expo / lax.optimization_barrier(jnp.sum(expo, axis=1, keepdims=True))
    grid = weights.reshape(weights.shape[0], SIDE, SIDE)
    centers = (jnp.arange(SIDE, dtype=jnp.float32) + 0.5) * (2.0 / SIDE) - 1.0
    vertical = lax.optimization_barrier(jnp.sum(lax.optimization_barrier(jnp.sum(grid, axis=2)) * centers, axis=1))
    horizontal = lax.optimization_barrier(jnp.sum(lax.optimization_barrier(jnp.sum(grid, axis=1)) * centers, axis=1))
    return (weights, vertical, horizontal)

def mix_block(padded, queries, inside, conv_kernel, norm_gain, w_in, w_out):
    length = padded.shape[1] - (KT - 1)
    read_part = jnp.zeros((padded.shape[0], length, C), jnp.float32)
    query_part = jnp.zeros((length, C), jnp.float32)
    for tap_index in range(KT):
        window = padded[:, tap_index:tap_index + length].astype(jnp.float32)
        read_part = read_part + conv_kernel[tap_index, :C] * window
        query_part = query_part + conv_kernel[tap_index, C:] * inside[tap_index:tap_index + length][:, None]
    query_part = query_part[None] * queries[:, None, :].astype(jnp.float32)
    blended = jnp.concatenate([read_part, query_part], axis=-1).reshape(-1, 2 * C)
    normed = (blended * lax.rsqrt(lax.optimization_barrier(jnp.mean(blended * blended, axis=1, keepdims=True)) + 1e-06) * norm_gain).astype(jnp.bfloat16)
    hidden = jnp.einsum('rm,hm->rh', normed.astype(jnp.float32), w_in.astype(jnp.float32))
    hidden = jax.nn.gelu(hidden).astype(jnp.bfloat16)
    update = jnp.dot(hidden, w_out, preferred_element_type=jnp.float32)
    result = (blended[:, :C] + update).astype(jnp.bfloat16)
    return result.reshape(padded.shape[0], length, C)

def reference(feature_maps, query_frame, query_pixel, conv_kernel, norm_gain, w_in, w_out):
    flat_maps = feature_maps.reshape(-1, C)
    flat_rows = (query_frame * HW + query_pixel[0] * SIDE + query_pixel[1]).astype(jnp.int32)
    queries = flat_maps[flat_rows]

    def first_pass(frame_map):
        weights, vertical, horizontal = soft_argmax(queries, frame_map)
        sampled = jnp.dot(weights.astype(jnp.bfloat16), frame_map, preferred_element_type=jnp.float32).astype(jnp.bfloat16)
        return (sampled, vertical, horizontal)
    sampled, vertical, horizontal = lax.map(first_pass, feature_maps)
    coarse_points = jnp.stack([vertical, horizontal], axis=0)
    half = (KT - 1) // 2
    by_track = jnp.transpose(sampled, (1, 0, 2))
    padded = jnp.pad(by_track, ((0, 0), (half, half), (0, 0)))
    inside = jnp.pad(jnp.ones((FRAMES,), jnp.float32), half)
    blocks = TRACKS // TR_DEV
    padded_blocks = padded.reshape(blocks, TR_DEV, FRAMES + 2 * half, C)
    query_blocks = queries.reshape(blocks, TR_DEV, C)

    def per_block(pair):
        return mix_block(pair[0], pair[1], inside, conv_kernel, norm_gain, w_in, w_out)
    updated = lax.map(per_block, (padded_blocks, query_blocks)).reshape(TRACKS, FRAMES, C)
    by_frame = jnp.transpose(updated, (1, 0, 2))

    def second_pass(pair):
        weights, vertical, horizontal = soft_argmax(pair[0], pair[1])
        return (vertical, horizontal)
    vertical, horizontal = lax.map(second_pass, (by_frame, feature_maps))
    refined_points = jnp.stack([vertical, horizontal], axis=0)
    return (coarse_points, refined_points)
```

```python
import jax
import jax.numpy as jnp
from jax import lax
from jax.sharding import Mesh
from jax.sharding import PartitionSpec as P

C = 256
SIDE = 64
KT = 3
FRAME = ("z", "x", "y")


def soft_argmax(queries, frame_map):
    scores = jnp.einsum(
        "tc,pc->tp", queries, frame_map, preferred_element_type=jnp.float32
    ) * C ** (-0.5)
    peak = jnp.max(scores, axis=1, keepdims=True)
    expo = jnp.exp(scores - peak)
    weights = expo / jnp.sum(expo, axis=1, keepdims=True)
    centers = (jnp.arange(SIDE, dtype=jnp.float32) + 0.5) * (2.0 / SIDE) - 1.0
    rows = jnp.repeat(centers, SIDE)
    columns = jnp.tile(centers, SIDE)
    vertical = jnp.sum(weights * rows, axis=1)
    horizontal = jnp.sum(weights * columns, axis=1)
    return (weights, vertical, horizontal)


def local(feature_maps, query_frame, query_pixel, conv_kernel, norm_gain, w_in, w_out):
    frames_here = feature_maps.shape[0]
    index = lax.axis_index(FRAME)
    count = lax.axis_size(FRAME)
    w_in = lax.all_gather(w_in, "track", axis=0, tiled=True)
    w_out = lax.all_gather(w_out, "track", axis=0, tiled=True)
    flat_maps = feature_maps.reshape(-1, C)
    offset_frame = query_frame - index * frames_here
    owned = (offset_frame >= 0) & (offset_frame < frames_here)
    flat_rows = (
        jnp.clip(offset_frame, 0, frames_here - 1) * (SIDE * SIDE)
        + query_pixel[0] * SIDE
        + query_pixel[1]
    )
    queries = jnp.where(owned[:, None], flat_maps[flat_rows], 0)
    for axis in ("z", "x", "y"):
        queries = lax.psum(queries, axis)
    sampled_list = []
    coarse = []
    for slot in range(frames_here):
        weights, vertical, horizontal = soft_argmax(queries, feature_maps[slot])
        sampled_list.append(
            jnp.dot(
                weights.astype(jnp.bfloat16),
                feature_maps[slot],
                preferred_element_type=jnp.float32,
            ).astype(jnp.bfloat16)
        )
        coarse.append(jnp.stack([vertical, horizontal], 0))
    from_left = lax.ppermute(sampled_list[-1], FRAME, [(i, i + 1) for i in range(count - 1)])
    from_right = lax.ppermute(sampled_list[0], FRAME, [(i + 1, i) for i in range(count - 1)])
    window = [from_left] + sampled_list + [from_right]
    inside = [(index > 0).astype(jnp.float32)] + [1.0] * frames_here
    inside += [(index < count - 1).astype(jnp.float32)]
    refined = []
    for slot in range(frames_here):
        read_part = 0.0
        query_part = 0.0
        for tap in range(KT):
            read_part = read_part + conv_kernel[tap, :C] * window[slot + tap].astype(jnp.float32)
            query_part = query_part + conv_kernel[tap, C:] * inside[slot + tap]
        query_part = query_part * queries.astype(jnp.float32)
        blended = jnp.concatenate([read_part, query_part], axis=-1)
        normed = (
            blended
            * lax.rsqrt(jnp.mean(blended * blended, axis=1, keepdims=True) + 1e-06)
            * norm_gain
        ).astype(jnp.bfloat16)
        hidden = jnp.einsum("rm,hm->rh", normed, w_in, preferred_element_type=jnp.float32)
        hidden = jax.nn.gelu(hidden).astype(jnp.bfloat16)
        update = jnp.dot(hidden, w_out, preferred_element_type=jnp.float32)
        updated = (blended[:, :C] + update).astype(jnp.bfloat16)
        _, vertical, horizontal = soft_argmax(updated, feature_maps[slot])
        refined.append(jnp.stack([vertical, horizontal], 0))
    return (jnp.stack(coarse, 1), jnp.stack(refined, 1))


def solution(mesh):
    sizes = {"y": 4, "x": 4}
    z = mesh.shape["frame"] // 16
    split = Mesh(
        mesh.devices.reshape(z, sizes["x"], sizes["y"], mesh.shape["track"]),
        ("z", "x", "y", "track"),
    )
    in_specs = (
        P(FRAME, None, None),
        P("track"),
        P(None, "track"),
        P(),
        P(),
        P("track", None),
        P("track", None),
    )
    out_specs = (P(None, FRAME, "track"), P(None, FRAME, "track"))
    return jax.shard_map(local, mesh=split, in_specs=in_specs, out_specs=out_specs, check_vma=False)
```
